32 devices in a mesh: groups: 2 (over y), row: 4 (over z), col: 4 (over x, core), rep: 1.
Axes of the slice: x: 2, y: 2, z: 4, core: 2. Of those that a mesh axis runs over, the one named last changes fastest.
Arguments:
- sequences: int32 [256, 160], P(('groups', 'rep')), parts along dimension 0, may hold values from 0 to 20
- seq_weights: float32 [256], P('groups'), parts along dimension 0, may hold values from 0.2 to 1
- fields: float32 [320, 21], P(('groups', 'row', 'col')), parts along dimension 0, may hold values from -3 to 3
- couplings: float32 [6720, 4, 4, 210], P(('groups', 'row', 'rep'), 'col'), parts along dimension 0, may hold values from -0.18 to 0.18
Outputs:
- new_couplings: float32 [6720, 4, 4, 210], P(('groups', 'row', 'rep'), 'col'), parts along dimension 0
- new_fields: float32 [320, 21], P(('groups', 'row', 'col')), parts along dimension 0
The draws below stay inside these ranges and needn't reach their ends.
There are 2 independent parts, one for each index of `groups`. The reference program is written for one: setup_inputs(seed, part) draws one part's arguments, and reference() takes and returns one part's arrays. A program takes and returns all parts, laid end to end along the dimension named above; each array names one. Nothing has to cross between parts.
All inputs are finite; a program needn't handle non-finite values.
Results may differ from the reference program's by a relative error of at most 0.0029.
Values may be sent and summed in bfloat16 or wider, within the bound.
A program may use at most 128 MiB of HBM per device.

```python
import math
import jax
import jax.numpy as jnp
from jax import lax

Q = 21
SITE_DEV = 10
STEPS = 2
L = 160
ORDER = 3360
M = 128
N_ROW = 4
N_COL = 4


def plant(array, own_key, low, top_value):
    longest = array.shape.index(max(array.shape))
    spots = []
    for shift in (0, 1):
        where = [jax.random.randint(jax.random.fold_in(own_key, axis), (), 0, length) for axis, length in enumerate(array.shape)]
        where[longest] = (where[longest] + shift) % array.shape[longest]
        spots.append(tuple(where))
    return array.at[spots[0]].set(low).at[spots[1]].set(top_value)


def block_levels(stream_key, dims, shards, least, largest):
    level, own = 1.0, jax.random.fold_in(stream_key, 6)
    for position, shards_of in shards:
        steps = jnp.exp(jax.random.uniform(jax.random.fold_in(own, position), (shards_of,), jnp.float32, least / len(shards), largest / len(shards)))
        level = level * jnp.repeat(steps, dims[position] // shards_of).reshape([-1 if axis == position else 1 for axis in range(len(dims))])
    return level


def noise(own_key, shape, deviation, bound, cuts=(), kind=jnp.bfloat16):
    gain = block_levels(own_key, shape, cuts, -0.22, 0.18) if cuts else 1.0
    array = jax.random.normal(own_key, shape, jnp.float32) * deviation * gain
    return jnp.minimum(jnp.maximum(array, -bound), bound).astype(kind)


def setup_inputs(seed: int = 0, part: int = 0) -> dict:
    arg_keys = jax.random.split(jax.random.key(seed), 5)
    part_keys = jax.random.split(jax.random.fold_in(arg_keys[4], part), 5)
    return {
        "sequences": plant(jax.random.randint(part_keys[0], (M, L), 0, Q), jax.random.fold_in(part_keys[0], 1), 0, Q - 1).astype(jnp.int32),
        "seq_weights": jnp.clip(jnp.exp(jax.random.uniform(part_keys[1], (M,), jnp.float32, math.log(0.2), math.log(1.0))), 0.2, 1.0),
        "fields": noise(part_keys[2], (L, Q), 0.5, 3.0, ((0, 16),), jnp.float32),
        "couplings": noise(part_keys[3], (ORDER, N_COL, N_ROW, SITE_DEV * Q), 0.03, 0.18, ((0, 4), (1, 4)), jnp.float32),
    }


learn_rate = 2.0
shrink = 0.02


def to_natural(couplings):
    order = couplings.shape[0]
    shaped = couplings.reshape(order, N_COL, N_ROW, SITE_DEV, Q)
    return shaped.transpose(0, 2, 1, 3, 4).reshape(order, order)


def to_folded(natural):
    order = natural.shape[0]
    shaped = natural.reshape(order, N_ROW, N_COL, SITE_DEV, Q)
    return shaped.transpose(0, 2, 1, 3, 4).reshape(order, N_COL, N_ROW, SITE_DEV * Q)


def block_mask(block_index, width):
    row_site = (block_index * width + jnp.arange(width, dtype=jnp.int32)) // Q
    col_site = jnp.arange(ORDER, dtype=jnp.int32) // Q
    return (row_site[:, None] != col_site[None, :]).astype(jnp.float32)


def reference(sequences, seq_weights, fields, couplings):
    width = ORDER // N_ROW
    precise = lax.Precision.HIGHEST
    onehot = (sequences[:, :, None] == jnp.arange(Q, dtype=jnp.int32)[None, None, :]).astype(jnp.float32)
    flat_onehot = onehot.reshape(M, ORDER)
    onehot_blocks = flat_onehot.reshape(M, N_ROW, width).transpose(1, 0, 2)
    block_ids = jnp.arange(N_ROW, dtype=jnp.int32)
    natural = to_natural(couplings).reshape(N_ROW, width, ORDER)
    natural = lax.map(lambda pair: pair[0] * block_mask(pair[1], width), (natural, block_ids))
    weight_total = jnp.sum(seq_weights)
    for iteration in range(STEPS):
        def logit_block(carry, inputs_pair):
            coupl_block, onehot_block = inputs_pair
            narrow = lax.optimization_barrier(coupl_block.astype(jnp.bfloat16))
            rounded = narrow.astype(jnp.float32)
            carry = carry + jnp.dot(onehot_block, rounded, precision=precise, preferred_element_type=jnp.float32)
            transposed_part = lax.dot_general(flat_onehot, rounded, (((1,), (1,)), ((), ())), precision=precise, preferred_element_type=jnp.float32)
            return carry, transposed_part

        direct, parts = lax.scan(logit_block, jnp.zeros((M, ORDER), jnp.float32), (natural, onehot_blocks))
        transposed = parts.transpose(1, 0, 2).reshape(M, ORDER)
        logits = (direct + transposed).reshape(M, L, Q) + fields[None]
        powers = jnp.exp(logits)
        probability = powers / jnp.sum(powers, axis=2, keepdims=True)
        resid = (seq_weights[:, None, None] * (probability - onehot)).astype(jnp.bfloat16)
        resid_wide = resid.astype(jnp.float32).reshape(M, ORDER)
        field_grad = jnp.sum(resid_wide, axis=0).reshape(L, Q)
        resid_blocks = resid_wide.reshape(M, N_ROW, width).transpose(1, 0, 2)

        def update(inputs_four):
            coupl_block, onehot_block, resid_block, block_index = inputs_four
            first = lax.dot_general(onehot_block, resid_wide, (((0,), (0,)), ((), ())), precision=precise, preferred_element_type=jnp.float32)
            second = lax.dot_general(resid_block, flat_onehot, (((0,), (0,)), ((), ())), precision=precise, preferred_element_type=jnp.float32)
            coupling_grad = block_mask(block_index, width) * (first + second)
            return coupl_block - learn_rate * (coupling_grad / weight_total + shrink * coupl_block)

        natural = lax.map(update, (natural, onehot_blocks, resid_blocks, block_ids))
        fields = fields - learn_rate * (field_grad / weight_total + shrink * fields)
    return to_folded(natural.reshape(ORDER, ORDER)), fields
```

```python
import functools
import jax
import jax.numpy as jnp
from jax import lax
from jax.experimental import pallas as pl
from jax.experimental.pallas import tpu as pltpu
from jax.sharding import PartitionSpec as P

STEPS = 2


learn_rate = 2.0
shrink = 0.02
decay = 1.0 - learn_rate * shrink
BF16 = jnp.bfloat16
F32 = jnp.float32
NN = (((1,), (0,)), ((), ()))
NT = (((1,), (1,)), ((), ()))


def dot(a, b, dims=NN, precision=None):
    return lax.dot_general(a, b, dims, precision=precision, preferred_element_type=F32)


def split(a):
    high = a.astype(BF16)
    return high, (a - high.astype(F32)).astype(BF16)


def site_of(shape, axis, states):
    position = lax.broadcasted_iota(jnp.int32, shape, axis).astype(F32)
    return jnp.floor((position + 0.5) * (1.0 / states))


def same_site(width, states):
    return (
        site_of((width, width), 0, states) == site_of((width, width), 1, states)
    ).astype(F32)


def state_of(width, states):
    position = lax.broadcasted_iota(jnp.int32, (1, width), 1).astype(F32)
    return position - states * site_of((1, width), 1, states)


def field_select(own_sites, states, width):
    level = lax.broadcasted_iota(jnp.int32, (states, width), 0).astype(F32)
    select = (level == state_of(width, states)).astype(F32)
    site = lax.broadcasted_iota(jnp.int32, (own_sites, width), 0).astype(F32)
    place = (site == site_of((own_sites, width), 1, states)).astype(F32)
    return select, place


def start_blocks(rows_of, slots, coupl_ref, held_ref, sem, width):
    copies = {}
    for near, far, source_row, source_col in rows_of:
        copy = pltpu.make_async_copy(
            coupl_ref.at[pl.ds(source_row * width, width), 0, source_col, :],
            held_ref.at[near, far],
            sem.at[near, far],
        )
        copy.start()
        copies[near, far] = copy
    return copies


def exchange_kernel(
    sizes,
    seq_ref, weight_ref, field_ref, coupl_ref,
    resid_col_ref, resid_row_ref, onehot_col_ref, onehot_row_ref, field_out_ref,
    held, narrow, onehot, send_d, recv_d, send_t, recv_t,
    near_send, near_recv, far_send, far_recv,
    load_sem, d_send, d_recv, t_send, t_recv, near_s, near_r, far_s, far_r,
    row_s, row_r, col_s, col_r,
):
    row_count, col_count, own_sites, states = sizes
    width = own_sites * states
    seq_count, site_count = seq_ref.shape
    row = lax.axis_index("row")
    col = lax.axis_index("col")
    rows = [lax.rem(row + k, row_count) for k in range(row_count)]
    cols = [lax.rem(col + k, col_count) for k in range(col_count)]
    order = [
        (c, r, cols[c], rows[r])
        for r in list(range(1, row_count)) + [0]
        for c in range(col_count)
    ]
    loads = start_blocks(order, None, coupl_ref, held, load_sem, width)

    barrier = pltpu.get_barrier_semaphore()
    for k in range(1, row_count):
        pl.semaphore_signal(barrier, inc=1, device_id={"row": rows[k]}, device_id_type=pl.DeviceIdType.MESH)
    for k in range(1, col_count):
        pl.semaphore_signal(barrier, inc=1, device_id={"col": cols[k]}, device_id_type=pl.DeviceIdType.MESH)

    codes = seq_ref[...].astype(F32).astype(BF16)
    levels = state_of(width, states)
    site = lax.broadcasted_iota(jnp.int32, (site_count, width), 0)
    lane_site = site_of((site_count, width), 1, states).astype(jnp.int32)

    def encode(block):
        pick = (site == lane_site + block * own_sites).astype(F32).astype(BF16)
        return (dot(codes, pick) == levels).astype(F32)

    blocks = row_count * col_count
    for block in range(blocks):
        onehot[block] = encode(block).astype(BF16)

    row_hot = [onehot[row * col_count + cols[c]] for c in range(col_count)]
    col_hot = [onehot[rows[r] * col_count + col] for r in range(row_count)]
    own_hot = row_hot[0]
    own_mask = same_site(width, states)

    def remote(source, target, send, receive, place):
        copy = pltpu.make_async_remote_copy(
            src_ref=source, dst_ref=target, send_sem=send, recv_sem=receive,
            device_id=place, device_id_type=pl.DeviceIdType.MESH,
        )
        copy.start()
        return copy

    pl.semaphore_wait(barrier, row_count + col_count - 2)
    copies = []
    direct = None
    for r in list(range(1, row_count)) + [0]:
        total = None
        for c in range(col_count):
            loads[c, r].wait()
            value = held[c, r]
            if c == 0 and r == 0:
                value = value * (1.0 - own_mask)
            value = value.astype(BF16)
            narrow[c, r] = value
            part = dot(row_hot[c], value)
            total = part if total is None else total + part
        if r:
            send_d[r - 1] = total.astype(BF16)
            copies.append(remote(
                send_d.at[r - 1], recv_d.at[r - 1], d_send.at[r - 1], d_recv.at[r - 1], {"row": rows[r]}
            ))
        else:
            direct = total
    transposed = None
    for c in list(range(1, col_count)) + [0]:
        total = None
        for r in range(row_count):
            part = dot(col_hot[r], narrow[c, r], NT)
            total = part if total is None else total + part
        if c:
            send_t[c - 1] = total.astype(BF16)
            copies.append(remote(
                send_t.at[c - 1], recv_t.at[c - 1], t_send.at[c - 1], t_recv.at[c - 1], {"col": cols[c]}
            ))
        else:
            transposed = total

    gram = jnp.zeros((seq_count, seq_count), F32)
    for block in range(blocks):
        gram += dot(onehot[block], onehot[block], NT)
    gram = split(gram)
    for r in range(row_count):
        onehot_col_ref[r] = onehot[r * col_count + col]
    for c in range(col_count):
        onehot_row_ref[c, 0:width] = onehot[row * col_count + c].astype(F32).T.astype(BF16)
    own_hot_t = own_hot.astype(F32).T.astype(BF16)
    own_f32 = own_hot.astype(F32)
    mask16 = own_mask.astype(BF16)
    weight_row = weight_ref[...]
    weight_total = jnp.sum(weight_row)
    diagonal = lax.broadcasted_iota(jnp.int32, (seq_count, seq_count), 0) == lax.broadcasted_iota(
        jnp.int32, (seq_count, seq_count), 1
    )
    weights = jnp.sum(jnp.where(diagonal, weight_row, 0.0), axis=1, keepdims=True)
    rate = learn_rate / weight_total
    select, place = field_select(own_sites, states, width)
    fields = jnp.sum(
        dot(field_ref[...], select, precision=lax.Precision.HIGHEST) * place, axis=0, keepdims=True
    )

    def residual(logits):
        powers = jnp.exp(logits)
        high, low = split(powers)
        sums = dot(high, mask16) + dot(low, mask16)
        return (weights * (powers / sums - own_f32)).astype(BF16)

    for copy in copies:
        copy.wait()
    logits = direct + transposed
    for k in range(row_count - 1):
        logits += recv_d[k].astype(F32)
    for k in range(col_count - 1):
        logits += recv_t[k].astype(F32)
    first = residual(logits + fields)

    cross = dot(own_hot, first, NT)
    near_send[...] = cross.astype(near_send.dtype)
    copies = [
        remote(near_send, near_recv.at[c - 1], near_s.at[c - 1], near_r.at[c - 1], {"col": cols[c]})
        for c in range(1, col_count)
    ]
    pairs = split(dot(own_hot_t, first) * own_mask)
    own_part = sum(dot(own_hot, half) + dot(own_hot, half, NT) for half in pairs)
    change = dot(gram[0], first) - own_part
    if site_count > 256:
        change += dot(gram[1], first)
    first_wide = first.astype(F32)
    fields = decay * fields - rate * jnp.sum(first_wide, axis=0, keepdims=True)
    base = fields + decay * logits - (2.0 * rate) * change
    for copy in copies:
        copy.wait()
    for k in range(col_count - 1):
        cross += near_recv[k].astype(F32)
    far_send[...] = cross.astype(far_send.dtype)
    copies = [
        remote(far_send, far_recv.at[r - 1], far_s.at[r - 1], far_r.at[r - 1], {"row": rows[r]})
        for r in range(1, row_count)
    ]
    for copy in copies:
        copy.wait()
    for k in range(row_count - 1):
        cross += far_recv[k].astype(F32)
    cross = split(cross)
    logits = base - (2.0 * rate) * (dot(cross[0], own_hot) + dot(cross[1], own_hot))
    second = residual(logits).astype(F32)
    both = decay * first_wide + second
    resid_col_ref[row] = both.astype(BF16)
    copies = [
        remote(resid_col_ref.at[row], resid_col_ref.at[row], row_s.at[r - 1], row_r.at[r - 1], {"row": rows[r]})
        for r in range(1, row_count)
    ]
    resid_row_ref[col, 0:width] = both.T.astype(BF16)
    if resid_row_ref.shape[1] > width:
        pad = resid_row_ref.shape[1] - width
        resid_row_ref[col, width:] = jnp.zeros((pad, seq_count), BF16)
    copies += [
        remote(resid_row_ref.at[col], resid_row_ref.at[col], col_s.at[c - 1], col_r.at[c - 1], {"col": cols[c]})
        for c in range(1, col_count)
    ]
    field_out_ref[...] = decay * fields - rate * jnp.sum(second, axis=0, keepdims=True)
    for copy in copies:
        copy.wait()


def update_kernel(
    sizes,
    weight_ref, field_ref, resid_col_ref, resid_row_ref, onehot_col_ref, onehot_row_ref, coupl_ref,
    out_ref, field_out_ref,
    held, load_sem, store_sem,
):
    row_count, col_count, own_sites, states = sizes
    width = own_sites * states
    row = lax.axis_index("row")
    col = lax.axis_index("col")
    rows = [lax.rem(row + k, row_count) for k in range(row_count)]
    cols = [lax.rem(col + k, col_count) for k in range(col_count)]
    order = [(c, r, cols[c], rows[r]) for c in range(col_count) for r in range(row_count)]
    loads = start_blocks(order, None, coupl_ref, held, load_sem, width)
    rate = learn_rate / jnp.sum(weight_ref[...])
    select, place = field_select(own_sites, states, width)
    field_out_ref[...] = dot(
        field_ref[...] * place, select, NT, precision=lax.Precision.HIGHEST
    )
    stores = []
    for c, r, source_row, source_col in order:
        left = jnp.concatenate(
            [onehot_row_ref[source_row, 0:width], resid_row_ref[source_row, 0:width]], axis=1
        )
        right = jnp.concatenate([resid_col_ref[source_col], onehot_col_ref[source_col]], axis=0)
        grad = dot(left, right)
        loads[c, r].wait()
        value = (decay * decay) * held[c, r] - rate * grad
        if c == 0 and r == 0:
            value = value * (1.0 - same_site(width, states))
        held[c, r] = value
        copy = pltpu.make_async_copy(
            held.at[c, r],
            out_ref.at[pl.ds(source_row * width, width), 0, source_col, :],
            store_sem.at[c, r],
        )
        copy.start()
        stores.append(copy)
    for copy in stores:
        copy.wait()


def fused_device(sequences, seq_weights, fields, couplings):
    row_count, col_count = lax.axis_size("row"), lax.axis_size("col")
    own_sites, states = fields.shape
    width = own_sites * states
    padded = -(-width // 16) * 16
    seq_count = sequences.shape[0]
    sizes = (row_count, col_count, own_sites, states)
    weights = seq_weights.reshape(1, seq_count)
    vmem = pl.BlockSpec(memory_space=pltpu.VMEM)
    hbm = pl.BlockSpec(memory_space=pl.ANY)
    dma = pltpu.SemaphoreType.DMA
    row_more, col_more = row_count - 1, col_count - 1
    square = (seq_count, seq_count)
    flat = (seq_count, width)
    resid_col, resid_row, onehot_col, onehot_row, field_flat = pl.pallas_call(
        functools.partial(exchange_kernel, sizes),
        out_shape=[
            jax.ShapeDtypeStruct((row_count, seq_count, width), BF16),
            jax.ShapeDtypeStruct((col_count, padded, seq_count), BF16),
            jax.ShapeDtypeStruct((row_count, seq_count, width), BF16),
            jax.ShapeDtypeStruct((col_count, padded, seq_count), BF16),
            jax.ShapeDtypeStruct((1, width), F32),
        ],
        in_specs=[vmem, vmem, vmem, hbm],
        out_specs=[vmem] * 5,
        scratch_shapes=[
            pltpu.VMEM((col_count, row_count, width, width), F32),
            pltpu.VMEM((col_count, row_count, width, width), BF16),
            pltpu.VMEM((row_count * col_count,) + flat, BF16),
            pltpu.VMEM((row_more,) + flat, BF16),
            pltpu.VMEM((row_more,) + flat, BF16),
            pltpu.VMEM((col_more,) + flat, BF16),
            pltpu.VMEM((col_more,) + flat, BF16),
            pltpu.VMEM(square, F32),
            pltpu.VMEM((col_more,) + square, F32),
            pltpu.VMEM(square, F32),
            pltpu.VMEM((row_more,) + square, F32),
            dma((col_count, row_count)),
            dma((row_more,)), dma((row_more,)), dma((col_more,)), dma((col_more,)),
            dma((col_more,)), dma((col_more,)), dma((row_more,)), dma((row_more,)),
            dma((row_more,)), dma((row_more,)), dma((col_more,)), dma((col_more,)),
        ],
        compiler_params=pltpu.CompilerParams(
            collective_id=0, has_side_effects=True, vmem_limit_bytes=40 * 1024 * 1024
        ),
        name="exchange",
    )(sequences, weights, fields, couplings)
    return pl.pallas_call(
        functools.partial(update_kernel, sizes),
        out_shape=[
            jax.ShapeDtypeStruct(couplings.shape, F32),
            jax.ShapeDtypeStruct(fields.shape, F32),
        ],
        in_specs=[vmem] * 6 + [hbm],
        out_specs=[hbm, vmem],
        scratch_shapes=[
            pltpu.VMEM((col_count, row_count, width, width), F32),
            dma((col_count, row_count)),
            dma((col_count, row_count)),
        ],
        compiler_params=pltpu.CompilerParams(vmem_limit_bytes=40 * 1024 * 1024),
        name="update",
    )(weights, field_flat, resid_col, resid_row, onehot_col, onehot_row, couplings)


def per_device(sequences, seq_weights, fields, couplings):
    half_rows = couplings.shape[0]
    row_count = couplings.shape[2]
    block_width = couplings.shape[3]
    own_sites = fields.shape[0]
    states = fields.shape[1]
    seq_count = sequences.shape[0]
    col_count = lax.axis_size("col")
    row_index = lax.axis_index("row")
    col_index = lax.axis_index("col")
    rep_index = lax.axis_index("rep")
    row_sites = own_sites * col_count
    row_width = row_sites * states
    global_rows = (
        row_index * row_width + rep_index * half_rows + jnp.arange(half_rows, dtype=jnp.int32)
    )
    row_site = global_rows // states
    block_pos = jnp.arange(row_count, dtype=jnp.int32)[:, None]
    within = jnp.arange(block_width, dtype=jnp.int32)[None, :] // states
    col_site = (block_pos * col_count + col_index) * own_sites + within
    off_diagonal = (row_site[:, None, None, None] != col_site[None, None, :, :]).astype(jnp.float32)
    coupl = couplings * off_diagonal
    weight_total = jnp.sum(seq_weights)
    own_weights = lax.dynamic_slice_in_dim(seq_weights, rep_index * seq_count, seq_count)
    seq_row = lax.dynamic_slice_in_dim(sequences, row_index * row_sites, row_sites, 1)
    seq_col = lax.dynamic_index_in_dim(
        sequences.reshape(seq_count, row_count, col_count, own_sites), col_index, 2, keepdims=False
    )
    seq_col = seq_col.reshape(seq_count, row_count * own_sites)
    seq_mine = lax.dynamic_slice_in_dim(seq_row, col_index * own_sites, own_sites, 1)
    levels = jnp.arange(states, dtype=jnp.int32)

    def encode(codes):
        return (
            (codes[:, :, None] == levels[None, None, :])
            .astype(jnp.bfloat16)
            .reshape(codes.shape[0], codes.shape[1] * states)
        )

    onehot_row = encode(seq_row)
    onehot_col = encode(seq_col)
    mine_onehot = (seq_mine.T[:, None, :] == levels[None, :, None]).astype(jnp.float32)
    every_row, every_col = (
        lax.all_gather(seq_row, "rep", axis=0, tiled=True),
        lax.all_gather(seq_col, "rep", axis=0, tiled=True),
    )
    wide_row = lax.dynamic_slice_in_dim(encode(every_row), rep_index * half_rows, half_rows, 1)
    wide_col = encode(every_col)
    for iteration in range(STEPS):
        narrow_rows = coupl.reshape(half_rows, row_count * block_width).astype(jnp.bfloat16)
        gathered = lax.all_gather(narrow_rows, "rep", axis=0, tiled=True)
        direct = lax.psum_scatter(
            lax.dot_general(
                gathered, onehot_row, (((0,), (1,)), ((), ())), preferred_element_type=jnp.float32
            ).astype(jnp.bfloat16),
            "row",
            scatter_dimension=0,
            tiled=True,
        ).astype(jnp.float32)
        transposed = lax.psum_scatter(
            lax.dot_general(
                gathered, onehot_col, (((1,), (1,)), ((), ())), preferred_element_type=jnp.float32
            ).astype(jnp.bfloat16),
            "col",
            scatter_dimension=0,
            tiled=True,
        ).astype(jnp.float32)
        logits = (direct + transposed).reshape(own_sites, states, seq_count) + fields[:, :, None]
        powers = jnp.exp(logits)
        probability = powers / jnp.sum(powers, axis=1, keepdims=True)
        resid = (own_weights[None, None, :] * (probability - mine_onehot)).astype(jnp.bfloat16)
        resid = resid.reshape(block_width, seq_count)
        all_resid = lax.all_gather(resid, "rep", axis=1, tiled=True)
        field_grad = jnp.sum(all_resid, axis=1, dtype=jnp.float32)
        by_row = lax.all_gather(all_resid, "row", axis=0, tiled=True)
        by_col = lax.all_gather(all_resid, "col", axis=0, tiled=True)
        mine_rows = lax.dynamic_slice_in_dim(by_col, rep_index * half_rows, half_rows, 0)
        first = lax.dot_general(
            wide_row, by_row, (((0,), (1,)), ((), ())), preferred_element_type=jnp.float32
        )
        second = lax.dot_general(
            mine_rows, wide_col, (((1,), (0,)), ((), ())), preferred_element_type=jnp.float32
        )
        coupling_grad = first + second
        coupling_grad = coupling_grad.reshape(half_rows, 1, row_count, block_width)
        coupl = coupl - learn_rate * (off_diagonal * coupling_grad / weight_total + shrink * coupl)
        fields = fields - learn_rate * (
            field_grad.reshape(own_sites, states) / weight_total + shrink * fields
        )
    return (coupl, fields)


def solution(mesh):
    in_specs = (
        P(("groups", "rep"), None),
        P("groups"),
        P(("groups", "row", "col"), None),
        P(("groups", "row", "rep"), "col", None, None),
    )
    out_specs = (P(("groups", "row", "rep"), "col", None, None), P(("groups", "row", "col"), None))
    fused = mesh.shape["rep"] == 1 and mesh.shape["row"] > 1 and mesh.shape["col"] > 1
    return jax.shard_map(
        fused_device if fused else per_device, mesh=mesh, in_specs=in_specs, out_specs=out_specs, check_vma=False
    )
```

```python
import functools
import jax
import jax.numpy as jnp
from jax import lax
from jax.experimental import pallas as pl
from jax.experimental.pallas import tpu as pltpu
from jax.sharding import PartitionSpec as P

STEPS = 2


learn_rate = 2.0
shrink = 0.02
decay = 1.0 - learn_rate * shrink
BF16 = jnp.bfloat16
F32 = jnp.float32
CROSS = jnp.bfloat16
NN = (((1,), (0,)), ((), ()))


def dot(a, b, dims=NN, precision=None):
    return lax.dot_general(a, b, dims, precision=precision, preferred_element_type=F32)


def split(a):
    high = a.astype(BF16)
    return high, (a - high.astype(F32)).astype(BF16)


def site_of(shape, axis, states):
    position = lax.broadcasted_iota(jnp.int32, shape, axis).astype(F32)
    return jnp.floor((position + 0.5) * (1.0 / states))


def state_of(shape, axis, states):
    position = lax.broadcasted_iota(jnp.int32, shape, axis).astype(F32)
    return position - states * site_of(shape, axis, states)


def same_site(width, states):
    shape = (width, width)
    return (site_of(shape, 0, states) == site_of(shape, 1, states)).astype(F32)


def diagonal_part(shape, col, own_sites, states):
    offset = (col * own_sites).astype(F32)
    return (site_of(shape, 0, states) + offset != site_of(shape, 1, states)).astype(F32)


def field_select(own_sites, states, width):
    level = lax.broadcasted_iota(jnp.int32, (width, states), 1).astype(F32)
    select = (level == state_of((width, states), 0, states)).astype(F32)
    site = lax.broadcasted_iota(jnp.int32, (width, own_sites), 1).astype(F32)
    place = (site == site_of((width, own_sites), 0, states)).astype(F32)
    return select, place


def encode_wide(codes_t, first_site, length, states):
    sites = codes_t.shape[0]
    shape = (length, sites)
    wanted = site_of(shape, 0, states).astype(jnp.int32) + first_site
    pick = (lax.broadcasted_iota(jnp.int32, shape, 1) == wanted).astype(F32).astype(BF16)
    level = state_of((length, 1), 0, states)
    return (dot(pick, codes_t) == level).astype(F32).astype(BF16)


def encode_tall(codes, first_site, length, states):
    sites = codes.shape[1]
    shape = (sites, length)
    wanted = site_of(shape, 1, states).astype(jnp.int32) + first_site
    pick = (lax.broadcasted_iota(jnp.int32, shape, 0) == wanted).astype(F32).astype(BF16)
    level = state_of((1, length), 1, states)
    return (dot(codes, pick) == level).astype(F32).astype(BF16)


def start_blocks(row_count, rows, coupl_ref, held_ref, sem):
    copies = {}
    for k in list(range(1, row_count)) + [0]:
        copy = pltpu.make_async_copy(coupl_ref.at[0, :, rows[k], :], held_ref.at[k], sem.at[k])
        copy.start()
        copies[k] = copy
    return copies


def exchange_kernel(
    sizes,
    seq_ref, weight_ref, field_ref, coupl_ref,
    held, first_col_ref, first_row_ref, second_col_ref, second_row_ref, onehot_col_ref, onehot_row_ref,
    field_out_ref,
    turned, own_t, send_d, recv_d, send_t, recv_t, first_own, second_own,
    near_send, near_recv, far_send, far_recv,
    load_sem, d_send, d_recv, t_send, t_recv, near_s, near_r, far_s, far_r,
    first_row_s, first_row_r, first_col_s, first_col_r,
    second_row_s, second_row_r, second_col_s, second_col_r,
):
    row_count, col_count, own_sites, states = sizes
    width = own_sites * states
    wide = width * col_count
    site_count, seq_count = seq_ref.shape
    row = lax.axis_index("row")
    col = lax.axis_index("col")
    rows = [lax.rem(row + k, row_count) for k in range(row_count)]
    cols = [lax.rem(col + k, col_count) for k in range(col_count)]
    loads = start_blocks(row_count, rows, coupl_ref, held, load_sem)

    mesh_id = pl.DeviceIdType.MESH
    barrier = pltpu.get_barrier_semaphore()
    for k in range(1, row_count):
        pl.semaphore_signal(barrier, inc=1, device_id={"row": rows[k]}, device_id_type=mesh_id)
    for k in range(1, col_count):
        pl.semaphore_signal(barrier, inc=1, device_id={"col": cols[k]}, device_id_type=mesh_id)

    def remote(source, target, send, receive, place):
        copy = pltpu.make_async_remote_copy(
            src_ref=source, dst_ref=target, send_sem=send, recv_sem=receive,
            device_id=place, device_id_type=mesh_id,
        )
        copy.start()
        return copy

    padded = send_d.shape[1]
    if padded > width:
        pad = padded - width
        for k in range(row_count - 1):
            send_d[k, width:] = jnp.zeros((pad, seq_count), BF16)
        for k in range(col_count):
            send_t[k, width:] = jnp.zeros((pad, seq_count), BF16)
        first_own[width:] = jnp.zeros((pad, seq_count), BF16)
        second_own[width:] = jnp.zeros((pad, seq_count), BF16)
    codes_f32 = seq_ref[...].astype(F32)
    codes_t = codes_f32.astype(BF16)
    codes = codes_f32.T.astype(BF16)
    row_hot_t = encode_wide(codes_t, row * (col_count * own_sites), wide, states)
    col_hot = [
        encode_tall(codes, (rows[k] * col_count + col) * own_sites, width, states)
        for k in range(row_count)
    ]
    apart = diagonal_part((width, wide), col, own_sites, states)

    pl.semaphore_wait(barrier, row_count + col_count - 2)
    copies = []
    direct = None
    tall = None
    for k in list(range(1, row_count)) + [0]:
        loads[k].wait()
        value = held[k]
        if k == 0:
            value = value * apart
            held[k] = value
        value = value.astype(BF16)
        part = dot(value, row_hot_t)
        if k:
            send_d[k - 1, 0:width] = part.astype(BF16)
            copies.append(remote(
                send_d.at[k - 1], recv_d.at[k - 1], d_send.at[k - 1], d_recv.at[k - 1], {"row": rows[k]}
            ))
        else:
            direct = part
        part = dot(col_hot[k], value)
        tall = part if tall is None else tall + part
    turned[...] = tall.T
    for c in range(col_count):
        block = turned[c * width : (c + 1) * width]
        own_t[c, 0:width] = block
        send_t[c, 0:width] = block.astype(BF16)
    for k in range(1, col_count):
        copies.append(remote(
            send_t.at[cols[k]], recv_t.at[k - 1], t_send.at[k - 1], t_recv.at[k - 1], {"col": cols[k]}
        ))

    gram = jnp.zeros((seq_count, seq_count), F32)
    for level in range(states):
        left = (codes.astype(F32) == level).astype(F32).astype(BF16)
        right = (codes_f32 == level).astype(F32).astype(BF16)
        gram += dot(left, right)
    gram = split(gram)
    for r in range(row_count):
        onehot_col_ref[r, 0:width] = encode_wide(
            codes_t, (r * col_count + col) * own_sites, width, states
        )
    onehot_row_ref[...] = encode_tall(codes, row * (col_count * own_sites), wide, states)
    own_hot = col_hot[0]
    own_hot_t = encode_wide(codes_t, (row * col_count + col) * own_sites, width, states)
    own_f32 = own_hot_t.astype(F32)
    own_mask = same_site(width, states)
    mask16 = own_mask.astype(BF16)
    weights = weight_ref[...]
    rate = learn_rate / jnp.sum(weights)
    select, place = field_select(own_sites, states, width)
    fields = jnp.sum(
        dot(place, field_ref[...], precision=lax.Precision.HIGHEST) * select, axis=1, keepdims=True
    )

    def residual(logits):
        powers = jnp.exp(logits)
        high, low = split(powers)
        sums = dot(mask16, high) + dot(mask16, low)
        return weights * (powers / sums - own_f32)

    for copy in copies:
        copy.wait()
    logits = direct + own_t[col, 0:width]
    for k in range(row_count - 1):
        logits += recv_d[k, 0:width].astype(F32)
    for k in range(col_count - 1):
        logits += recv_t[k, 0:width].astype(F32)
    first = residual(logits + fields).astype(BF16)
    first_own[0:width] = first
    first_wide = first.astype(F32)
    first_tall = first_wide.T.astype(BF16)

    cross = dot(first_tall, own_hot_t)
    near_send[...] = cross.astype(near_send.dtype)
    copies = [
        remote(near_send, near_recv.at[k - 1], near_s.at[k - 1], near_r.at[k - 1], {"col": cols[k]})
        for k in range(1, col_count)
    ]
    pairs = split((dot(own_hot_t, first_tall) + dot(first, own_hot)) * own_mask)
    change = dot(first, gram[0]) - dot(pairs[0], own_hot_t) - dot(pairs[1], own_hot_t)
    if site_count > 256:
        change += dot(first, gram[1])
    fields = decay * fields - rate * jnp.sum(first_wide, axis=1, keepdims=True)
    base = fields + decay * logits - (2.0 * rate) * change
    for copy in copies:
        copy.wait()
    for k in range(col_count - 1):
        cross += near_recv[k].astype(F32)
    far_send[...] = cross.astype(far_send.dtype)
    copies = [
        remote(far_send, far_recv.at[k - 1], far_s.at[k - 1], far_r.at[k - 1], {"row": rows[k]})
        for k in range(1, row_count)
    ]
    far_copies = copies
    copies = [
        remote(first_own, first_row_ref.at[col], first_col_s.at[k - 1], first_col_r.at[k - 1], {"col": cols[k]})
        for k in range(1, col_count)
    ]
    for copy in far_copies:
        copy.wait()
    copies += [
        remote(first_own, first_col_ref.at[row], first_row_s.at[k - 1], first_row_r.at[k - 1], {"row": rows[k]})
        for k in range(1, row_count)
    ]
    for k in range(row_count - 1):
        cross += far_recv[k].astype(F32)
    cross = split(cross)
    logits = base - (2.0 * rate) * (dot(own_hot_t, cross[0]) + dot(own_hot_t, cross[1]))
    second = residual(logits).astype(BF16)
    second_own[0:width] = second
    second = second.astype(F32)
    copies += [
        remote(second_own, second_col_ref.at[row], second_row_s.at[k - 1], second_row_r.at[k - 1], {"row": rows[k]})
        for k in range(1, row_count)
    ]
    copies += [
        remote(second_own, second_row_ref.at[col], second_col_s.at[k - 1], second_col_r.at[k - 1], {"col": cols[k]})
        for k in range(1, col_count)
    ]
    for own_ref, by_col, by_row in (
        (first_own, first_col_ref, first_row_ref), (second_own, second_col_ref, second_row_ref)
    ):
        own = own_ref[...]
        by_col[row] = own
        by_row[col] = own
    field_out_ref[...] = decay * fields - rate * jnp.sum(second, axis=1, keepdims=True)
    for copy in copies:
        copy.wait()


def update_kernel(
    sizes,
    weight_ref, field_ref, held_ref, first_col_ref, first_row_ref, second_col_ref, second_row_ref,
    onehot_col_ref, onehot_row_ref,
    out_ref, field_out_ref,
    result, stacked, store_sem,
):
    row_count, col_count, own_sites, states = sizes
    width = own_sites * states
    wide = width * col_count
    row = lax.axis_index("row")
    col = lax.axis_index("col")
    rows = [lax.rem(row + k, row_count) for k in range(row_count)]
    rate = learn_rate / jnp.sum(weight_ref[...])
    select, place = field_select(own_sites, states, width)
    field_out_ref[...] = lax.dot_general(
        place, field_ref[...] * select, (((0,), (0,)), ((), ())),
        precision=lax.Precision.HIGHEST, preferred_element_type=F32,
    )
    rights = []
    for by_row in (first_row_ref, second_row_ref):
        for c in range(col_count):
            stacked[c * width : (c + 1) * width] = by_row[c, 0:width].astype(F32)
        rights.append(jnp.concatenate([stacked[...].T.astype(BF16), onehot_row_ref[...]], axis=0))
    stores = []
    for k in range(row_count):
        value = (decay * decay) * held_ref[k]
        hot = onehot_col_ref[rows[k], 0:width]
        for by_col, right, scale in (
            (first_col_ref, rights[0], decay), (second_col_ref, rights[1], 1.0)
        ):
            left = jnp.concatenate([hot, by_col[rows[k], 0:width]], axis=1)
            value = value - (scale * rate) * dot(left, right)
        if k == 0:
            value = value * diagonal_part((width, wide), col, own_sites, states)
        result[k] = value
        copy = pltpu.make_async_copy(result.at[k], out_ref.at[0, :, rows[k], :], store_sem.at[k])
        copy.start()
        stores.append(copy)
    for copy in stores:
        copy.wait()


def fused_device(sequences, seq_weights, fields, couplings):
    row_count, col_count = lax.axis_size("row"), lax.axis_size("col")
    own_sites, states = fields.shape
    width = own_sites * states
    wide = width * col_count
    padded = -(-width // 16) * 16
    seq_count = sequences.shape[0]
    sizes = (row_count, col_count, own_sites, states)
    weights = seq_weights.reshape(1, seq_count)
    turned = couplings.transpose(1, 3, 2, 0)
    vmem = pl.BlockSpec(memory_space=pltpu.VMEM)
    hbm = pl.BlockSpec(memory_space=pltpu.HBM)
    dma = pltpu.SemaphoreType.DMA
    row_more, col_more = row_count - 1, col_count - 1
    square = (seq_count, seq_count)
    flat = (padded, seq_count)
    held, *parts, field_flat = pl.pallas_call(
        functools.partial(exchange_kernel, sizes),
        out_shape=[
            jax.ShapeDtypeStruct((row_count, width, wide), F32),
            jax.ShapeDtypeStruct((row_count,) + flat, BF16),
            jax.ShapeDtypeStruct((col_count,) + flat, BF16),
            jax.ShapeDtypeStruct((row_count,) + flat, BF16),
            jax.ShapeDtypeStruct((col_count,) + flat, BF16),
            jax.ShapeDtypeStruct((row_count,) + flat, BF16),
            jax.ShapeDtypeStruct((seq_count, wide), BF16),
            jax.ShapeDtypeStruct((width, 1), F32),
        ],
        in_specs=[vmem, vmem, vmem, hbm],
        out_specs=[vmem] * 8,
        scratch_shapes=[
            pltpu.VMEM((wide, seq_count), F32),
            pltpu.VMEM((col_count,) + flat, F32),
            pltpu.VMEM((row_more,) + flat, BF16),
            pltpu.VMEM((row_more,) + flat, BF16),
            pltpu.VMEM((col_count,) + flat, BF16),
            pltpu.VMEM((col_more,) + flat, BF16),
            pltpu.VMEM(flat, BF16),
            pltpu.VMEM(flat, BF16),
            pltpu.VMEM(square, CROSS),
            pltpu.VMEM((col_more,) + square, CROSS),
            pltpu.VMEM(square, CROSS),
            pltpu.VMEM((row_more,) + square, CROSS),
            dma((row_count,)),
            dma((row_more,)), dma((row_more,)), dma((col_more,)), dma((col_more,)),
            dma((col_more,)), dma((col_more,)), dma((row_more,)), dma((row_more,)),
            dma((row_more,)), dma((row_more,)), dma((col_more,)), dma((col_more,)),
            dma((row_more,)), dma((row_more,)), dma((col_more,)), dma((col_more,)),
        ],
        compiler_params=pltpu.CompilerParams(
            collective_id=0, has_side_effects=True, vmem_limit_bytes=58 * 1024 * 1024
        ),
        name="exchange",
    )(sequences.T, weights, fields, turned)
    out, new_fields = pl.pallas_call(
        functools.partial(update_kernel, sizes),
        out_shape=[
            jax.ShapeDtypeStruct(turned.shape, F32),
            jax.ShapeDtypeStruct(fields.shape, F32),
        ],
        in_specs=[vmem] * 9,
        out_specs=[hbm, vmem],
        scratch_shapes=[
            pltpu.VMEM((row_count, width, wide), F32),
            pltpu.VMEM((wide, seq_count), F32),
            dma((row_count,)),
        ],
        compiler_params=pltpu.CompilerParams(vmem_limit_bytes=40 * 1024 * 1024),
        name="update",
    )(weights, field_flat, held, *parts)
    return (out.transpose(3, 0, 2, 1), new_fields)


def per_device(sequences, seq_weights, fields, couplings):
    half_rows = couplings.shape[0]
    row_count = couplings.shape[2]
    block_width = couplings.shape[3]
    own_sites = fields.shape[0]
    states = fields.shape[1]
    seq_count = sequences.shape[0]
    col_count = lax.axis_size("col")
    row_index = lax.axis_index("row")
    col_index = lax.axis_index("col")
    rep_index = lax.axis_index("rep")
    row_sites = own_sites * col_count
    row_width = row_sites * states
    global_rows = (
        row_index * row_width + rep_index * half_rows + jnp.arange(half_rows, dtype=jnp.int32)
    )
    row_site = global_rows // states
    block_pos = jnp.arange(row_count, dtype=jnp.int32)[:, None]
    within = jnp.arange(block_width, dtype=jnp.int32)[None, :] // states
    col_site = (block_pos * col_count + col_index) * own_sites + within
    off_diagonal = (row_site[:, None, None, None] != col_site[None, None, :, :]).astype(jnp.float32)
    coupl = couplings * off_diagonal
    weight_total = jnp.sum(seq_weights)
    own_weights = lax.dynamic_slice_in_dim(seq_weights, rep_index * seq_count, seq_count)
    seq_row = lax.dynamic_slice_in_dim(sequences, row_index * row_sites, row_sites, 1)
    seq_col = lax.dynamic_index_in_dim(
        sequences.reshape(seq_count, row_count, col_count, own_sites), col_index, 2, keepdims=False
    )
    seq_col = seq_col.reshape(seq_count, row_count * own_sites)
    seq_mine = lax.dynamic_slice_in_dim(seq_row, col_index * own_sites, own_sites, 1)
    levels = jnp.arange(states, dtype=jnp.int32)

    def encode(codes):
        return (
            (codes[:, :, None] == levels[None, None, :])
            .astype(jnp.bfloat16)
            .reshape(codes.shape[0], codes.shape[1] * states)
        )

    onehot_row = encode(seq_row)
    onehot_col = encode(seq_col)
    mine_onehot = (seq_mine.T[:, None, :] == levels[None, :, None]).astype(jnp.float32)
    every_row, every_col = (
        lax.all_gather(seq_row, "rep", axis=0, tiled=True),
        lax.all_gather(seq_col, "rep", axis=0, tiled=True),
    )
    wide_row = lax.dynamic_slice_in_dim(encode(every_row), rep_index * half_rows, half_rows, 1)
    wide_col = encode(every_col)
    for iteration in range(STEPS):
        narrow_rows = coupl.reshape(half_rows, row_count * block_width).astype(jnp.bfloat16)
        gathered = lax.all_gather(narrow_rows, "rep", axis=0, tiled=True)
        direct = lax.psum_scatter(
            lax.dot_general(
                gathered, onehot_row, (((0,), (1,)), ((), ())), preferred_element_type=jnp.float32
            ).astype(jnp.bfloat16),
            "row",
            scatter_dimension=0,
            tiled=True,
        ).astype(jnp.float32)
        transposed = lax.psum_scatter(
            lax.dot_general(
                gathered, onehot_col, (((1,), (1,)), ((), ())), preferred_element_type=jnp.float32
            ).astype(jnp.bfloat16),
            "col",
            scatter_dimension=0,
            tiled=True,
        ).astype(jnp.float32)
        logits = (direct + transposed).reshape(own_sites, states, seq_count) + fields[:, :, None]
        powers = jnp.exp(logits)
        probability = powers / jnp.sum(powers, axis=1, keepdims=True)
        resid = (own_weights[None, None, :] * (probability - mine_onehot)).astype(jnp.bfloat16)
        resid = resid.reshape(block_width, seq_count)
        all_resid = lax.all_gather(resid, "rep", axis=1, tiled=True)
        field_grad = jnp.sum(all_resid, axis=1, dtype=jnp.float32)
        by_row = lax.all_gather(all_resid, "row", axis=0, tiled=True)
        by_col = lax.all_gather(all_resid, "col", axis=0, tiled=True)
        mine_rows = lax.dynamic_slice_in_dim(by_col, rep_index * half_rows, half_rows, 0)
        first = lax.dot_general(
            wide_row, by_row, (((0,), (1,)), ((), ())), preferred_element_type=jnp.float32
        )
        second = lax.dot_general(
            mine_rows, wide_col, (((1,), (0,)), ((), ())), preferred_element_type=jnp.float32
        )
        coupling_grad = first + second
        coupling_grad = coupling_grad.reshape(half_rows, 1, row_count, block_width)
        coupl = coupl - learn_rate * (off_diagonal * coupling_grad / weight_total + shrink * coupl)
        fields = fields - learn_rate * (
            field_grad.reshape(own_sites, states) / weight_total + shrink * fields
        )
    return (coupl, fields)


def solution(mesh):
    in_specs = (
        P(("groups", "rep"), None),
        P("groups"),
        P(("groups", "row", "col"), None),
        P(("groups", "row", "rep"), "col", None, None),
    )
    out_specs = (P(("groups", "row", "rep"), "col", None, None), P(("groups", "row", "col"), None))
    fused = mesh.shape["rep"] == 1 and mesh.shape["row"] > 1 and mesh.shape["col"] > 1
    return jax.shard_map(
        fused_device if fused else per_device, mesh=mesh, in_specs=in_specs, out_specs=out_specs, check_vma=False
    )
```

```python
import functools
import jax
import jax.numpy as jnp
from jax import lax
from jax.experimental import pallas as pl
from jax.experimental.pallas import tpu as pltpu
from jax.sharding import PartitionSpec as P

STEPS = 2


learn_rate = 2.0
shrink = 0.02
decay = 1.0 - learn_rate * shrink
BF16 = jnp.bfloat16
F32 = jnp.float32
CROSS = jnp.bfloat16
NN = (((1,), (0,)), ((), ()))


def dot(a, b, dims=NN, precision=None):
    return lax.dot_general(a, b, dims, precision=precision, preferred_element_type=F32)


def split(a):
    high = a.astype(BF16)
    return high, (a - high.astype(F32)).astype(BF16)


def site_of(shape, axis, states):
    position = lax.broadcasted_iota(jnp.int32, shape, axis).astype(F32)
    return jnp.floor((position + 0.5) * (1.0 / states))


def state_of(shape, axis, states):
    position = lax.broadcasted_iota(jnp.int32, shape, axis).astype(F32)
    return position - states * site_of(shape, axis, states)


def same_site(width, states):
    shape = (width, width)
    return (site_of(shape, 0, states) == site_of(shape, 1, states)).astype(F32)


def diagonal_part(shape, col, own_sites, states):
    offset = (col * own_sites).astype(F32)
    return (site_of(shape, 0, states) + offset != site_of(shape, 1, states)).astype(F32)


def field_select(own_sites, states, width):
    level = lax.broadcasted_iota(jnp.int32, (width, states), 1).astype(F32)
    select = (level == state_of((width, states), 0, states)).astype(F32)
    site = lax.broadcasted_iota(jnp.int32, (width, own_sites), 1).astype(F32)
    place = (site == site_of((width, own_sites), 0, states)).astype(F32)
    return select, place


def encode_wide(codes_t, first_site, length, states):
    sites = codes_t.shape[0]
    shape = (length, sites)
    wanted = site_of(shape, 0, states).astype(jnp.int32) + first_site
    pick = (lax.broadcasted_iota(jnp.int32, shape, 1) == wanted).astype(F32).astype(BF16)
    level = state_of((length, 1), 0, states)
    return (dot(pick, codes_t) == level).astype(F32).astype(BF16)


def encode_tall(codes, first_site, length, states):
    sites = codes.shape[1]
    shape = (sites, length)
    wanted = site_of(shape, 1, states).astype(jnp.int32) + first_site
    pick = (lax.broadcasted_iota(jnp.int32, shape, 0) == wanted).astype(F32).astype(BF16)
    level = state_of((1, length), 1, states)
    return (dot(codes, pick) == level).astype(F32).astype(BF16)


def start_blocks(row_count, rows, coupl_ref, held_ref, sem):
    copies = {}
    for k in list(range(1, row_count)) + [0]:
        copy = pltpu.make_async_copy(coupl_ref.at[0, :, rows[k], :], held_ref.at[k], sem.at[k])
        copy.start()
        copies[k] = copy
    return copies


def exchange_kernel(
    sizes,
    seq_ref, weight_ref, field_ref, coupl_ref,
    held, first_col_ref, first_row_ref, second_col_ref, second_row_ref, onehot_col_ref, onehot_row_ref,
    field_out_ref,
    turned, own_t, send_d, recv_d, send_t, recv_t, first_own, second_own,
    far_send, far_recv,
    load_sem, d_send, d_recv, t_send, t_recv, far_s, far_r,
    first_row_s, first_row_r, first_col_s, first_col_r,
    second_row_s, second_row_r, second_col_s, second_col_r,
):
    row_count, col_count, own_sites, states = sizes
    width = own_sites * states
    wide = width * col_count
    site_count, seq_count = seq_ref.shape
    row = lax.axis_index("row")
    col = lax.axis_index("col")
    rows = [lax.rem(row + k, row_count) for k in range(row_count)]
    cols = [lax.rem(col + k, col_count) for k in range(col_count)]
    loads = start_blocks(row_count, rows, coupl_ref, held, load_sem)

    mesh_id = pl.DeviceIdType.MESH
    barrier = pltpu.get_barrier_semaphore()
    for k in range(1, row_count):
        pl.semaphore_signal(barrier, inc=1, device_id={"row": rows[k]}, device_id_type=mesh_id)
    for k in range(1, col_count):
        pl.semaphore_signal(barrier, inc=1, device_id={"col": cols[k]}, device_id_type=mesh_id)

    def remote(source, target, send, receive, place):
        copy = pltpu.make_async_remote_copy(
            src_ref=source, dst_ref=target, send_sem=send, recv_sem=receive,
            device_id=place, device_id_type=mesh_id,
        )
        copy.start()
        return copy

    padded = send_d.shape[1]
    if padded > width:
        pad = padded - width
        for k in range(row_count - 1):
            send_d[k, width:] = jnp.zeros((pad, seq_count), BF16)
        for k in range(col_count):
            send_t[k, width:] = jnp.zeros((pad, seq_count), BF16)
        first_own[width:] = jnp.zeros((pad, seq_count), BF16)
        second_own[width:] = jnp.zeros((pad, seq_count), BF16)
    codes_f32 = seq_ref[...].astype(F32)
    codes_t = codes_f32.astype(BF16)
    codes = codes_f32.T.astype(BF16)
    row_hot_t = encode_wide(codes_t, row * (col_count * own_sites), wide, states)
    col_hot = [
        encode_tall(codes, (rows[k] * col_count + col) * own_sites, width, states)
        for k in range(row_count)
    ]
    apart = diagonal_part((width, wide), col, own_sites, states)

    pl.semaphore_wait(barrier, row_count + col_count - 2)
    copies = []
    direct = None
    tall = None
    for k in list(range(1, row_count)) + [0]:
        loads[k].wait()
        value = held[k]
        if k == 0:
            value = value * apart
            held[k] = value
        value = value.astype(BF16)
        part = dot(value, row_hot_t)
        if k:
            send_d[k - 1, 0:width] = part.astype(BF16)
            copies.append(remote(
                send_d.at[k - 1], recv_d.at[k - 1], d_send.at[k - 1], d_recv.at[k - 1], {"row": rows[k]}
            ))
        else:
            direct = part
        part = dot(col_hot[k], value)
        tall = part if tall is None else tall + part
    turned[0:wide] = tall.T
    for c in range(col_count):
        block = turned[c * width : (c + 1) * width]
        own_t[c, 0:width] = block
        send_t[c, 0:width] = block.astype(BF16)
    for k in range(1, col_count):
        copies.append(remote(
            send_t.at[cols[k]], recv_t.at[k - 1], t_send.at[k - 1], t_recv.at[k - 1], {"col": cols[k]}
        ))

    gram = jnp.zeros((seq_count, seq_count), F32)
    for level in range(states):
        left = (codes.astype(F32) == level).astype(F32).astype(BF16)
        right = (codes_f32 == level).astype(F32).astype(BF16)
        gram += dot(left, right)
    gram = split(gram)
    for r in range(row_count):
        onehot_col_ref[r, 0:width] = encode_wide(
            codes_t, (r * col_count + col) * own_sites, width, states
        )
    onehot_row_ref[...] = encode_tall(codes, row * (col_count * own_sites), wide, states)
    own_hot = col_hot[0]
    own_hot_t = encode_wide(codes_t, (row * col_count + col) * own_sites, width, states)
    own_f32 = own_hot_t.astype(F32)
    own_mask = same_site(width, states)
    mask16 = own_mask.astype(BF16)
    weights = weight_ref[...]
    rate = learn_rate / jnp.sum(weights)
    select, place = field_select(own_sites, states, width)
    fields = jnp.sum(
        dot(place, field_ref[...], precision=lax.Precision.HIGHEST) * select, axis=1, keepdims=True
    )

    def residual(logits):
        powers = jnp.exp(logits)
        high, low = split(powers)
        sums = dot(mask16, high) + dot(mask16, low)
        return weights * (powers / sums - own_f32)

    for copy in copies:
        copy.wait()
    logits = direct + own_t[col, 0:width]
    for k in range(row_count - 1):
        logits += recv_d[k, 0:width].astype(F32)
    for k in range(col_count - 1):
        logits += recv_t[k, 0:width].astype(F32)
    first = residual(logits + fields).astype(BF16)
    first_own[0:width] = first
    first_wide = first.astype(F32)
    first_tall = first_wide.T.astype(BF16)

    near_copies = [
        remote(first_own, first_row_ref.at[col], first_col_s.at[k - 1], first_col_r.at[k - 1], {"col": cols[k]})
        for k in range(1, col_count)
    ]
    copies = [
        remote(first_own, first_col_ref.at[row], first_row_s.at[k - 1], first_row_r.at[k - 1], {"row": rows[k]})
        for k in range(1, row_count)
    ]
    own = first_own[...]
    first_row_ref[col] = own
    first_col_ref[row] = own
    pairs = split((dot(own_hot_t, first_tall) + dot(first, own_hot)) * own_mask)
    change = dot(first, gram[0]) - dot(pairs[0], own_hot_t) - dot(pairs[1], own_hot_t)
    if site_count > 256:
        change += dot(first, gram[1])
    fields = decay * fields - rate * jnp.sum(first_wide, axis=1, keepdims=True)
    base = fields + decay * logits - (2.0 * rate) * change
    for copy in near_copies:
        copy.wait()
    for c in range(col_count):
        turned[c * width : (c + 1) * width] = first_row_ref[c, 0:width].astype(F32)
    cross = dot(turned[0:wide].T.astype(BF16), row_hot_t)
    far_send[...] = cross.astype(far_send.dtype)
    far_copies = [
        remote(far_send, far_recv.at[k - 1], far_s.at[k - 1], far_r.at[k - 1], {"row": rows[k]})
        for k in range(1, row_count)
    ]
    for copy in far_copies:
        copy.wait()
    for k in range(row_count - 1):
        cross += far_recv[k].astype(F32)
    cross = split(cross)
    logits = base - (2.0 * rate) * (dot(own_hot_t, cross[0]) + dot(own_hot_t, cross[1]))
    second = residual(logits).astype(BF16)
    second_own[0:width] = second
    second = second.astype(F32)
    copies += [
        remote(second_own, second_col_ref.at[row], second_row_s.at[k - 1], second_row_r.at[k - 1], {"row": rows[k]})
        for k in range(1, row_count)
    ]
    copies += [
        remote(second_own, second_row_ref.at[col], second_col_s.at[k - 1], second_col_r.at[k - 1], {"col": cols[k]})
        for k in range(1, col_count)
    ]
    own = second_own[...]
    second_col_ref[row] = own
    second_row_ref[col] = own
    field_out_ref[...] = decay * fields - rate * jnp.sum(second, axis=1, keepdims=True)
    for copy in copies:
        copy.wait()


def update_kernel(
    sizes,
    weight_ref, field_ref, held_ref, first_col_ref, first_row_ref, second_col_ref, second_row_ref,
    onehot_col_ref, onehot_row_ref,
    out_ref, field_out_ref,
    result, stacked, store_sem,
):
    row_count, col_count, own_sites, states = sizes
    width = own_sites * states
    wide = width * col_count
    row = lax.axis_index("row")
    col = lax.axis_index("col")
    rows = [lax.rem(row + k, row_count) for k in range(row_count)]
    rate = learn_rate / jnp.sum(weight_ref[...])
    select, place = field_select(own_sites, states, width)
    field_out_ref[...] = lax.dot_general(
        place, field_ref[...] * select, (((0,), (0,)), ((), ())),
        precision=lax.Precision.HIGHEST, preferred_element_type=F32,
    )
    rights = []
    for by_row in (first_row_ref, second_row_ref):
        for c in range(col_count):
            stacked[c * width : (c + 1) * width] = by_row[c, 0:width].astype(F32)
        rights.append(jnp.concatenate([stacked[0:wide].T.astype(BF16), onehot_row_ref[...]], axis=0))
    stores = []
    for k in range(row_count):
        value = (decay * decay) * held_ref[k]
        hot = onehot_col_ref[rows[k], 0:width]
        for by_col, right, scale in (
            (first_col_ref, rights[0], decay), (second_col_ref, rights[1], 1.0)
        ):
            left = jnp.concatenate([hot, by_col[rows[k], 0:width]], axis=1)
            value = value - (scale * rate) * dot(left, right)
        if k == 0:
            value = value * diagonal_part((width, wide), col, own_sites, states)
        result[k] = value
        copy = pltpu.make_async_copy(result.at[k], out_ref.at[0, :, rows[k], :], store_sem.at[k])
        copy.start()
        stores.append(copy)
    for copy in stores:
        copy.wait()


def fused_device(sequences, seq_weights, fields, couplings):
    row_count, col_count = lax.axis_size("row"), lax.axis_size("col")
    own_sites, states = fields.shape
    width = own_sites * states
    wide = width * col_count
    padded = -(-width // 16) * 16
    seq_count = sequences.shape[0]
    sizes = (row_count, col_count, own_sites, states)
    weights = seq_weights.reshape(1, seq_count)
    turned = couplings.transpose(1, 3, 2, 0)
    vmem = pl.BlockSpec(memory_space=pltpu.VMEM)
    hbm = pl.BlockSpec(memory_space=pl.ANY)
    dma = pltpu.SemaphoreType.DMA
    row_more, col_more = row_count - 1, col_count - 1
    square = (seq_count, seq_count)
    flat = (padded, seq_count)
    held, *parts, field_flat = pl.pallas_call(
        functools.partial(exchange_kernel, sizes),
        out_shape=[
            jax.ShapeDtypeStruct((row_count, width, wide), F32),
            jax.ShapeDtypeStruct((row_count,) + flat, BF16),
            jax.ShapeDtypeStruct((col_count,) + flat, BF16),
            jax.ShapeDtypeStruct((row_count,) + flat, BF16),
            jax.ShapeDtypeStruct((col_count,) + flat, BF16),
            jax.ShapeDtypeStruct((row_count,) + flat, BF16),
            jax.ShapeDtypeStruct((seq_count, wide), BF16),
            jax.ShapeDtypeStruct((width, 1), F32),
        ],
        in_specs=[vmem, vmem, vmem, hbm],
        out_specs=[vmem] * 8,
        scratch_shapes=[
            pltpu.VMEM((wide + 24, seq_count), F32),
            pltpu.VMEM((col_count,) + flat, F32),
            pltpu.VMEM((row_more,) + flat, BF16),
            pltpu.VMEM((row_more,) + flat, BF16),
            pltpu.VMEM((col_count,) + flat, BF16),
            pltpu.VMEM((col_more,) + flat, BF16),
            pltpu.VMEM(flat, BF16),
            pltpu.VMEM(flat, BF16),
            pltpu.VMEM(square, CROSS),
            pltpu.VMEM((row_more,) + square, CROSS),
            dma((row_count,)),
            dma((row_more,)), dma((row_more,)), dma((col_more,)), dma((col_more,)),
            dma((row_more,)), dma((row_more,)),
            dma((row_more,)), dma((row_more,)), dma((col_more,)), dma((col_more,)),
            dma((row_more,)), dma((row_more,)), dma((col_more,)), dma((col_more,)),
        ],
        compiler_params=pltpu.CompilerParams(
            collective_id=0, has_side_effects=True, vmem_limit_bytes=46 * 1024 * 1024
        ),
        name="exchange",
    )(sequences.T, weights, fields, turned)
    out, new_fields = pl.pallas_call(
        functools.partial(update_kernel, sizes),
        out_shape=[
            jax.ShapeDtypeStruct(turned.shape, F32),
            jax.ShapeDtypeStruct(fields.shape, F32),
        ],
        in_specs=[vmem] * 9,
        out_specs=[hbm, vmem],
        scratch_shapes=[
            pltpu.VMEM((row_count, width, wide), F32),
            pltpu.VMEM((wide + 24, seq_count), F32),
            dma((row_count,)),
        ],
        compiler_params=pltpu.CompilerParams(vmem_limit_bytes=40 * 1024 * 1024),
        name="update",
    )(weights, field_flat, held, *parts)
    return (out.transpose(3, 0, 2, 1), new_fields)


def per_device(sequences, seq_weights, fields, couplings):
    half_rows = couplings.shape[0]
    row_count = couplings.shape[2]
    block_width = couplings.shape[3]
    own_sites = fields.shape[0]
    states = fields.shape[1]
    seq_count = sequences.shape[0]
    col_count = lax.axis_size("col")
    row_index = lax.axis_index("row")
    col_index = lax.axis_index("col")
    rep_index = lax.axis_index("rep")
    row_sites = own_sites * col_count
    row_width = row_sites * states
    global_rows = (
        row_index * row_width + rep_index * half_rows + jnp.arange(half_rows, dtype=jnp.int32)
    )
    row_site = global_rows // states
    block_pos = jnp.arange(row_count, dtype=jnp.int32)[:, None]
    within = jnp.arange(block_width, dtype=jnp.int32)[None, :] // states
    col_site = (block_pos * col_count + col_index) * own_sites + within
    off_diagonal = (row_site[:, None, None, None] != col_site[None, None, :, :]).astype(jnp.float32)
    coupl = couplings * off_diagonal
    weight_total = jnp.sum(seq_weights)
    own_weights = lax.dynamic_slice_in_dim(seq_weights, rep_index * seq_count, seq_count)
    seq_row = lax.dynamic_slice_in_dim(sequences, row_index * row_sites, row_sites, 1)
    seq_col = lax.dynamic_index_in_dim(
        sequences.reshape(seq_count, row_count, col_count, own_sites), col_index, 2, keepdims=False
    )
    seq_col = seq_col.reshape(seq_count, row_count * own_sites)
    seq_mine = lax.dynamic_slice_in_dim(seq_row, col_index * own_sites, own_sites, 1)
    levels = jnp.arange(states, dtype=jnp.int32)

    def encode(codes):
        return (
            (codes[:, :, None] == levels[None, None, :])
            .astype(jnp.bfloat16)
            .reshape(codes.shape[0], codes.shape[1] * states)
        )

    onehot_row = encode(seq_row)
    onehot_col = encode(seq_col)
    mine_onehot = (seq_mine.T[:, None, :] == levels[None, :, None]).astype(jnp.float32)
    every_row, every_col = (
        lax.all_gather(seq_row, "rep", axis=0, tiled=True),
        lax.all_gather(seq_col, "rep", axis=0, tiled=True),
    )
    wide_row = lax.dynamic_slice_in_dim(encode(every_row), rep_index * half_rows, half_rows, 1)
    wide_col = encode(every_col)
    for iteration in range(STEPS):
        narrow_rows = coupl.reshape(half_rows, row_count * block_width).astype(jnp.bfloat16)
        gathered = lax.all_gather(narrow_rows, "rep", axis=0, tiled=True)
        direct = lax.psum_scatter(
            lax.dot_general(
                gathered, onehot_row, (((0,), (1,)), ((), ())), preferred_element_type=jnp.float32
            ).astype(jnp.bfloat16),
            "row",
            scatter_dimension=0,
            tiled=True,
        ).astype(jnp.float32)
        transposed = lax.psum_scatter(
            lax.dot_general(
                gathered, onehot_col, (((1,), (1,)), ((), ())), preferred_element_type=jnp.float32
            ).astype(jnp.bfloat16),
            "col",
            scatter_dimension=0,
            tiled=True,
        ).astype(jnp.float32)
        logits = (direct + transposed).reshape(own_sites, states, seq_count) + fields[:, :, None]
        powers = jnp.exp(logits)
        probability = powers / jnp.sum(powers, axis=1, keepdims=True)
        resid = (own_weights[None, None, :] * (probability - mine_onehot)).astype(jnp.bfloat16)
        resid = resid.reshape(block_width, seq_count)
        all_resid = lax.all_gather(resid, "rep", axis=1, tiled=True)
        field_grad = jnp.sum(all_resid, axis=1, dtype=jnp.float32)
        by_row = lax.all_gather(all_resid, "row", axis=0, tiled=True)
        by_col = lax.all_gather(all_resid, "col", axis=0, tiled=True)
        mine_rows = lax.dynamic_slice_in_dim(by_col, rep_index * half_rows, half_rows, 0)
        first = lax.dot_general(
            wide_row, by_row, (((0,), (1,)), ((), ())), preferred_element_type=jnp.float32
        )
        second = lax.dot_general(
            mine_rows, wide_col, (((1,), (0,)), ((), ())), preferred_element_type=jnp.float32
        )
        coupling_grad = first + second
        coupling_grad = coupling_grad.reshape(half_rows, 1, row_count, block_width)
        coupl = coupl - learn_rate * (off_diagonal * coupling_grad / weight_total + shrink * coupl)
        fields = fields - learn_rate * (
            field_grad.reshape(own_sites, states) / weight_total + shrink * fields
        )
    return (coupl, fields)


def solution(mesh):
    in_specs = (
        P(("groups", "rep"), None),
        P("groups"),
        P(("groups", "row", "col"), None),
        P(("groups", "row", "rep"), "col", None, None),
    )
    out_specs = (P(("groups", "row", "rep"), "col", None, None), P(("groups", "row", "col"), None))
    fused = mesh.shape["rep"] == 1 and mesh.shape["row"] > 1 and mesh.shape["col"] > 1
    return jax.shard_map(
        fused_device if fused else per_device, mesh=mesh, in_specs=in_specs, out_specs=out_specs, check_vma=False
    )
```
